32 devices in a mesh: seq: 8 (over y, x, core), head: 4 (over z).
Axes of the slice: x: 2, y: 2, z: 4, core: 2. Of those that a mesh axis runs over, the one named last changes fastest.
Arguments:
- queries: bfloat16 [4096, 4096], P(('seq', 'head')), may hold values from -1.796875 to 1.796875
- keys: bfloat16 [4096, 4096], P(('seq', 'head')), may hold values from -1.796875 to 1.796875
- values: bfloat16 [4096, 4096], P(('seq', 'head')), may hold values from -1.796875 to 1.796875
- grad_out: bfloat16 [4096, 4096], P(('seq', 'head')), may hold values from -0.09375 to 0.09375
Outputs:
- grad_q: bfloat16 [4096, 4096], P(('seq', 'head'))
- grad_k: bfloat16 [4096, 4096], P(('seq', 'head'))
- grad_v: bfloat16 [4096, 4096], P(('seq', 'head'))
The draws below stay inside these ranges and needn't reach their ends.
All inputs are finite; a program needn't handle non-finite values.
Results may differ from the reference program's by a relative error of at most 0.0025.
Values may be sent and summed in bfloat16 or wider, within the bound.
A program may use at most 128 MiB of HBM per device.

```python
import jax
import jax.numpy as jnp
from jax import lax

HEADS = 32
DK = 128
SPAN = 512
SEQ = 4096
N_SEQ = 8


def levels(stream_key, shape, split, low, high):
    factor_of, own = 1.0, jax.random.fold_in(stream_key, 6)
    for dim, shards_of in split:
        steps = jnp.exp(jax.random.uniform(jax.random.fold_in(own, dim), (shards_of,), jnp.float32, low / len(split), high / len(split)))
        factor_of = factor_of * jnp.repeat(steps, shape[dim] // shards_of).reshape([-1 if axis == dim else 1 for axis in range(len(shape))])
    return factor_of


def normal_values(own_key, shape, deviation, limit, shards=(), dtype=jnp.bfloat16):
    level = levels(own_key, shape, shards, -0.22, 0.18) if shards else 1.0
    values = jax.random.normal(own_key, shape, jnp.float32) * deviation * level
    return jnp.minimum(jnp.maximum(values, -limit), limit).astype(dtype)


def setup_inputs(seed: int = 0) -> dict:
    splits = jax.random.split(jax.random.key(seed), 5)
    queries = normal_values(splits[0], (SEQ, HEADS * DK), 0.3, 1.796875, ((0, 32),))
    keys = normal_values(splits[1], (SEQ, HEADS * DK), 0.3, 1.796875, ((0, 32),))
    values = normal_values(splits[2], (SEQ, HEADS * DK), 0.3, 1.796875, ((0, 32),))
    grad_out = normal_values(splits[3], (SEQ, HEADS * DK), (SEQ ** -0.5), 0.09375, ((0, 32),))
    return dict(queries=queries, keys=keys, values=values, grad_out=grad_out)


def one_head(block):
    query, key, value, grad = block
    qf = query.astype(jnp.float32)
    kf = key.astype(jnp.float32)
    vf = value.astype(jnp.float32)
    gf = grad.astype(jnp.float32)
    high = lax.Precision.HIGHEST
    key_state = jnp.einsum('ncd,nce->nde', kf, vf, precision=high)
    grad_state = jnp.einsum('ncd,nce->nde', qf, gf, precision=high)
    prefix = jnp.cumsum(key_state, axis=0) - key_state
    suffix = jnp.sum(grad_state, axis=0)[None] - jnp.cumsum(grad_state, axis=0)
    position = lax.iota(jnp.int32, SPAN)
    causal = position[:, None] >= position[None, :]
    weights_a = jnp.where(causal[None], jnp.einsum('nte,nse->nts', gf, vf, precision=high), 0.0).astype(jnp.bfloat16).astype(jnp.float32)
    weights_b = jnp.where(causal[None], jnp.einsum('ntd,nsd->nts', qf, kf, precision=high), 0.0).astype(jnp.bfloat16).astype(jnp.float32)
    grad_query = jnp.einsum('nts,nsd->ntd', weights_a, kf, precision=high) + jnp.einsum('nte,nde->ntd', gf, prefix, precision=high)
    grad_key = jnp.einsum('nts,ntd->nsd', weights_a, qf, precision=high) + jnp.einsum('nse,nde->nsd', vf, suffix, precision=high)
    grad_value = jnp.einsum('nts,ntd->nsd', weights_b, gf, precision=high) + jnp.einsum('nsd,nde->nse', kf, suffix, precision=high)
    return (grad_query.astype(jnp.bfloat16), grad_key.astype(jnp.bfloat16), grad_value.astype(jnp.bfloat16))


def split_heads(array):
    return jnp.transpose(array.reshape(N_SEQ, SPAN, HEADS, DK), (2, 0, 1, 3))


def join_heads(array):
    return jnp.transpose(array, (1, 2, 0, 3)).reshape(N_SEQ * SPAN, HEADS * DK)


def reference(queries, keys, values, grad_out):
    blocks = (split_heads(queries), split_heads(keys), split_heads(values), split_heads(grad_out))
    grad_query, grad_key, grad_value = lax.map(one_head, blocks)
    return (join_heads(grad_query), join_heads(grad_key), join_heads(grad_value))
```

```python
import functools

import jax
import jax.numpy as jnp
from jax import lax
from jax.experimental import pallas as pl
from jax.experimental.pallas import tpu as pltpu
from jax.sharding import PartitionSpec as P

DK = 128
PIECE = 1
MESH = pl.DeviceIdType.MESH
NT = (((1,), (1,)), ((), ()))
TN = (((0,), (0,)), ((), ()))
NN = (((1,), (0,)), ((), ()))


def dot(left, right, dims):
    return lax.dot_general(left, right, dims, preferred_element_type=jnp.float32)


def enc(x):
    return (x * jnp.abs(x) * (x * x)).astype(jnp.bfloat16)


def dec(y):
    y = y.astype(jnp.float32)
    root = jnp.sqrt(jnp.sqrt(jnp.abs(y)))
    return jnp.where(y < 0, -root, root)


def split(x):
    high = x.astype(jnp.bfloat16)
    return high, (x - high.astype(jnp.float32)).astype(jnp.bfloat16)


def kernel(
    ns, nz, q, k, v, o, gq, gk, gv,
    base, s_right, r_right, s_left, r_left, own, total, carried, s_seq, r_seq, p_left, p_right, r_back,
    right_s, right_r, left_s, left_r, seq_s, seq_r, back_left, back_right, back_r,
):
    n, z = lax.axis_index("seq"), lax.axis_index("head")
    rounds = ns.bit_length() - 1
    group = base.shape[1] // nz
    pieces = r_right.shape[1]
    first, last = z == 0, z == nz - 1
    gathered = nz - 1

    def later_bit(r):
        return lax.rem(lax.div(n, 1 << r), 2)

    def partner(r):
        return n + (1 - 2 * later_bit(r)) * (1 << r)

    def remote(src, dst, send, recv, where):
        return pltpu.make_async_remote_copy(
            src_ref=src, dst_ref=dst, send_sem=send, recv_sem=recv, device_id=where, device_id_type=MESH
        )

    def go_right(g, c):
        return remote(s_right.at[g, c], r_right.at[g, c], right_s.at[g, c], right_r.at[g, c], {"head": z + 1})

    def go_left(g, c):
        return remote(s_left.at[g, c], r_left.at[g, c], left_s.at[g, c], left_r.at[g, c], {"head": z - 1})

    def go_seq(r, c):
        return remote(s_seq.at[r, c], r_seq.at[r, c], seq_s.at[r, c], seq_r.at[r, c], {"seq": partner(r)})

    def back_to_left(src, g, c):
        return remote(src, r_back.at[g, c], back_left.at[g, c], back_r.at[g, c], {"head": z - 1})

    def back_to_right(src, g, c):
        return remote(src, r_back.at[g, c], back_right.at[g, c], back_r.at[g, c], {"head": z + 1})

    barrier = pltpu.get_barrier_semaphore()

    @pl.when(z > 0)
    def _():
        pl.semaphore_signal(barrier, inc=1, device_id={"head": z - 1}, device_id_type=MESH)

    @pl.when(z < nz - 1)
    def _():
        pl.semaphore_signal(barrier, inc=1, device_id={"head": z + 1}, device_id_type=MESH)

    for r in range(rounds):
        pl.semaphore_signal(barrier, inc=1, device_id={"seq": partner(r)}, device_id_type=MESH)

    @pl.when(first)
    def _():
        r_right[...] = jnp.zeros_like(r_right)

    @pl.when(last)
    def _():
        r_left[...] = jnp.zeros_like(r_left)

    r_back[z] = jnp.zeros(r_back.shape[1:], r_back.dtype)

    neighbours = (z > 0).astype(jnp.int32) + (z < nz - 1).astype(jnp.int32)
    pl.semaphore_wait(barrier, rounds + neighbours)

    def block(ref, h):
        return ref[:, pl.ds(pl.multiple_of(h * DK, DK), DK)]

    def states(h):
        return dot(block(k, h), block(v, h), TN), dot(block(q, h), block(o, h), TN)

    def right_stage(g, c):
        @pl.when(z > 0)
        def _():
            go_right(g, c).wait_recv()

        for j in range(PIECE):
            h = g * group + c * PIECE + j
            key_state, grad_state = states(h)
            before_key, before_grad = dec(r_right[g, c, j]), dec(r_right[g, c, PIECE + j])
            upto_key, upto_grad = before_key + key_state, before_grad + grad_state
            s_right[g, c, j] = enc(upto_key)
            s_right[g, c, PIECE + j] = enc(upto_grad)
            base[0, h] = before_key
            base[1, h] = -upto_grad
        go_right(g, c).start()

    def left_stage(g, c):
        @pl.when(z < nz - 1)
        def _():
            go_left(g, c).wait_recv()

        for j in range(PIECE):
            h = g * group + c * PIECE + j
            key_state, grad_state = states(h)
            after_key, after_grad = dec(r_left[g, c, j]), dec(r_left[g, c, PIECE + j])
            from_key, from_grad = after_key + key_state, after_grad + grad_state
            s_left[g, c, j] = enc(from_key)
            s_left[g, c, PIECE + j] = enc(from_grad)
            base[0, h] = -from_key
            base[1, h] = after_grad
        go_left(g, c).start()

    def owner_stage(c):
        @pl.when(z > 0)
        def _():
            go_right(z, c).wait_recv()

        @pl.when(z < nz - 1)
        def _():
            go_left(z, c).wait_recv()

        for j in range(PIECE):
            h, i = z * group + c * PIECE + j, c * PIECE + j
            key_state, grad_state = states(h)
            before_key, after_grad = dec(r_right[z, c, j]), dec(r_left[z, c, PIECE + j])
            base[0, h] = before_key
            base[1, h] = after_grad
            sums = (
                before_key + key_state + dec(r_left[z, c, j]),
                dec(r_right[z, c, PIECE + j]) + grad_state + after_grad,
            )
            for s in range(2):
                own[s, i] = sums[s]
                total[s, i] = sums[s]
                carried[s, i] = jnp.zeros((DK, DK), jnp.float32)
                s_seq[0, c, s * PIECE + j] = enc(sums[s])
        go_seq(0, c).start()

    def seq_stage(r, c):
        go_seq(r - 1, c).wait_recv()
        partner_earlier = later_bit(r - 1).astype(jnp.float32)
        for j in range(PIECE):
            h, i = z * group + c * PIECE + j, c * PIECE + j
            got_key, got_grad = dec(r_seq[r - 1, c, j]), dec(r_seq[r - 1, c, PIECE + j])
            new_key = carried[0, i] + got_key * partner_earlier
            new_grad = carried[1, i] + got_grad * (1.0 - partner_earlier)
            if r < rounds:
                carried[0, i] = new_key
                carried[1, i] = new_grad
                total_key, total_grad = total[0, i] + got_key, total[1, i] + got_grad
                total[0, i] = total_key
                total[1, i] = total_grad
                s_seq[r, c, j] = enc(total_key)
                s_seq[r, c, PIECE + j] = enc(total_grad)
            else:
                base[0, h] += new_key
                base[1, h] += new_grad
                p_left[c, j] = enc(new_key)
                p_left[c, PIECE + j] = enc(new_grad + own[1, i])
                p_right[c, j] = enc(new_key + own[0, i])
                p_right[c, PIECE + j] = enc(new_grad)
        if r < rounds:
            go_seq(r, c).start()
        else:
            @pl.when(z > 0)
            def _():
                back_to_left(p_left.at[c], z, c).start()

            @pl.when(z < nz - 1)
            def _():
                back_to_right(p_right.at[c], z, c).start()

    def relay_left(g, c):
        back_to_left(r_back.at[g, c], g, c).wait_recv()

        @pl.when(z > 0)
        def _():
            back_to_left(r_back.at[g, c], g, c).start()

    def relay_right(g, c):
        back_to_right(r_back.at[g, c], g, c).wait_recv()

        @pl.when(z < nz - 1)
        def _():
            back_to_right(r_back.at[g, c], g, c).start()

    rows = q.shape[0]
    causal = lax.broadcasted_iota(jnp.int32, (rows, rows), 0) >= lax.broadcasted_iota(jnp.int32, (rows, rows), 1)

    def finish(g, c):
        for j in range(PIECE):
            h = g * group + c * PIECE + j
            qh, kh, vh, oh = block(q, h), block(k, h), block(v, h), block(o, h)
            prefix_high, prefix_low = split(base[0, h] + dec(r_back[g, c, j]))
            suffix_high, suffix_low = split(base[1, h] + dec(r_back[g, c, PIECE + j]))
            weights_a = jnp.where(causal, dot(oh, vh, NT), 0.0).astype(jnp.bfloat16)
            weights_b = jnp.where(causal, dot(qh, kh, NT), 0.0).astype(jnp.bfloat16)
            grad_q = dot(weights_a, kh, NN) + dot(oh, prefix_high, NT) + dot(oh, prefix_low, NT)
            grad_k = dot(weights_a, qh, TN) + dot(vh, suffix_high, NT) + dot(vh, suffix_low, NT)
            grad_v = dot(weights_b, oh, TN) + dot(kh, suffix_high, NN) + dot(kh, suffix_low, NN)
            columns = pl.ds(pl.multiple_of(h * DK, DK), DK)
            gq[:, columns] = grad_q.astype(jnp.bfloat16)
            gk[:, columns] = grad_k.astype(jnp.bfloat16)
            gv[:, columns] = grad_v.astype(jnp.bfloat16)

    def valid(c):
        return (c >= 0) & (c < pieces)

    def step(t, carry):
        for g in range(nz):
            cl = t - (gathered + rounds) - (g - z)

            @pl.when((g > z) & valid(cl))
            def _():
                relay_left(g, cl)

            cr = t - (gathered + rounds) - (z - g)

            @pl.when((g < z) & valid(cr))
            def _():
                relay_right(g, cr)

        for r in reversed(range(1, rounds + 1)):
            cs = t - gathered - r

            @pl.when(valid(cs))
            def _():
                seq_stage(r, cs)

        co = t - gathered

        @pl.when(valid(co))
        def _():
            owner_stage(co)

        c_right, c_left = t - z, t - (nz - 1 - z)
        for g in range(nz):
            far = nz - 1 - g

            @pl.when((far > z) & valid(c_right))
            def _():
                right_stage(far, c_right)

            @pl.when((g < z) & valid(c_left))
            def _():
                left_stage(g, c_left)

        cf = t - (2 * gathered + rounds)

        @pl.when(valid(cf))
        def _():
            lax.fori_loop(0, nz, lambda g, u: (finish(g, cf), u)[1], 0)

        return carry

    lax.fori_loop(0, pieces + 2 * gathered + rounds, step, 0)

    def drain(c, carry):
        for g in range(nz):
            @pl.when(g > z)
            def _():
                go_right(g, c).wait_send()

            @pl.when(g < z)
            def _():
                go_left(g, c).wait_send()

            @pl.when((g >= z) & (z > 0))
            def _():
                back_to_left(r_back.at[g, c], g, c).wait_send()

            @pl.when((g <= z) & (z < nz - 1))
            def _():
                back_to_right(r_back.at[g, c], g, c).wait_send()

        for r in range(rounds):
            go_seq(r, c).wait_send()
        return carry

    lax.fori_loop(0, pieces, drain, 0)


def body(ns, nz, queries, keys, values, grad_out):
    heads = queries.shape[1] // DK
    group = heads // nz
    pieces = group // PIECE
    rounds = ns.bit_length() - 1
    moved = (pieces, 2 * PIECE, DK, DK)

    def bf(*lead):
        return pltpu.VMEM(lead + moved, jnp.bfloat16)

    def f32(count):
        return pltpu.VMEM((2, count, DK, DK), jnp.float32)

    by_group = pltpu.SemaphoreType.DMA((nz, pieces))
    by_round = pltpu.SemaphoreType.DMA((rounds, pieces))
    return pl.pallas_call(
        functools.partial(kernel, ns, nz),
        out_shape=[jax.ShapeDtypeStruct(queries.shape, jnp.bfloat16)] * 3,
        in_specs=[pl.BlockSpec(memory_space=pltpu.VMEM)] * 4,
        out_specs=[pl.BlockSpec(memory_space=pltpu.VMEM)] * 3,
        scratch_shapes=[
            f32(heads), bf(nz), bf(nz), bf(nz), bf(nz), f32(group), f32(group), f32(group),
            bf(rounds), bf(rounds), bf(), bf(), bf(nz),
            by_group, by_group, by_group, by_group, by_round, by_round, by_group, by_group, by_group,
        ],
        compiler_params=pltpu.CompilerParams(
            collective_id=0, has_side_effects=True, vmem_limit_bytes=48 * 1024 * 1024
        ),
    )(queries, keys, values, grad_out)


def solution(mesh):
    ns, nz = mesh.shape["seq"], mesh.shape["head"]
    spec = P(("seq", "head"), None)
    return jax.shard_map(
        functools.partial(body, ns, nz), mesh=mesh, in_specs=(spec,) * 4, out_specs=(spec,) * 3, check_vma=False
    )
```

```python
import functools

import jax
import jax.numpy as jnp
from jax import lax
from jax.experimental import pallas as pl
from jax.experimental.pallas import tpu as pltpu
from jax.sharding import PartitionSpec as P

DK = 128
PIECE = 1
SKEW = 3
MESH = pl.DeviceIdType.MESH
NT = (((1,), (1,)), ((), ()))
TN = (((0,), (0,)), ((), ()))
NN = (((1,), (0,)), ((), ()))


def dot(left, right, dims):
    return lax.dot_general(left, right, dims, preferred_element_type=jnp.float32)


def enc(x):
    return (x * jnp.abs(x) * (x * x)).astype(jnp.bfloat16)


def dec(y):
    y = y.astype(jnp.float32)
    root = jnp.sqrt(jnp.sqrt(jnp.abs(y)))
    return jnp.where(y < 0, -root, root)


def split(x):
    high = x.astype(jnp.bfloat16)
    return high, (x - high.astype(jnp.float32)).astype(jnp.bfloat16)


def kernel(
    ns, nz, q, k, v, o, gq, gk, gv,
    base, s_right, r_right, s_left, r_left, own, total, carried, s_seq, r_seq, result, r_back,
    right_s, right_r, left_s, left_r, seq_s, seq_r, back_s, back_r,
):
    n, z = lax.axis_index("seq"), lax.axis_index("head")
    rounds = ns.bit_length() - 1
    group = base.shape[1] // 2
    mine = (z == nz - 1).astype(jnp.int32)
    pieces = r_right.shape[0]
    first, last = z == 0, z == nz - 1
    gathered = nz - 1

    def later_bit(r):
        return lax.rem(lax.div(n, 1 << r), 2)

    def partner(r):
        return n + (1 - 2 * later_bit(r)) * (1 << r)

    def remote(src, dst, send, recv, where):
        return pltpu.make_async_remote_copy(
            src_ref=src, dst_ref=dst, send_sem=send, recv_sem=recv, device_id=where, device_id_type=MESH
        )

    def go_right(c):
        return remote(s_right.at[c], r_right.at[c], right_s.at[c], right_r.at[c], {"head": z + 1})

    def go_left(c):
        return remote(s_left.at[c], r_left.at[c], left_s.at[c], left_r.at[c], {"head": z - 1})

    def go_seq(r, c):
        return remote(s_seq.at[r, c], r_seq.at[r, c], seq_s.at[r, c], seq_r.at[r, c], {"seq": partner(r)})

    def back_to_left(src, c):
        return remote(src, r_back.at[1, c], back_s.at[1, c], back_r.at[1, c], {"head": z - 1})

    def back_to_right(src, c):
        return remote(src, r_back.at[0, c], back_s.at[0, c], back_r.at[0, c], {"head": z + 1})

    barrier = pltpu.get_barrier_semaphore()

    @pl.when(z > 0)
    def _():
        pl.semaphore_signal(barrier, inc=1, device_id={"head": z - 1}, device_id_type=MESH)

    @pl.when(z < nz - 1)
    def _():
        pl.semaphore_signal(barrier, inc=1, device_id={"head": z + 1}, device_id_type=MESH)

    for r in range(rounds):
        pl.semaphore_signal(barrier, inc=1, device_id={"seq": partner(r)}, device_id_type=MESH)

    @pl.when(first)
    def _():
        r_right[...] = jnp.zeros_like(r_right)

    @pl.when(last)
    def _():
        r_left[...] = jnp.zeros_like(r_left)

    @pl.when(first)
    def _():
        r_back[0] = jnp.zeros(r_back.shape[1:], r_back.dtype)

    @pl.when(last)
    def _():
        r_back[1] = jnp.zeros(r_back.shape[1:], r_back.dtype)

    neighbours = (z > 0).astype(jnp.int32) + (z < nz - 1).astype(jnp.int32)
    pl.semaphore_wait(barrier, rounds + neighbours)

    def block(ref, h):
        return ref[:, pl.ds(pl.multiple_of(h * DK, DK), DK)]

    def states(h):
        return dot(block(k, h), block(v, h), TN), dot(block(q, h), block(o, h), TN)

    def right_stage(c):
        @pl.when(z > 0)
        def _():
            go_right(c).wait_recv()

        for j in range(PIECE):
            h = group + c * PIECE + j
            key_state, grad_state = states(h)
            before_key, before_grad = dec(r_right[c, j]), dec(r_right[c, PIECE + j])
            upto_key, upto_grad = before_key + key_state, before_grad + grad_state
            s_right[c, j] = enc(upto_key)
            s_right[c, PIECE + j] = enc(upto_grad)
            base[0, h] = before_key
            base[1, h] = -upto_grad
        go_right(c).start()

    def left_stage(c):
        @pl.when(z < nz - 1)
        def _():
            go_left(c).wait_recv()

        for j in range(PIECE):
            h = c * PIECE + j
            key_state, grad_state = states(h)
            after_key, after_grad = dec(r_left[c, j]), dec(r_left[c, PIECE + j])
            from_key, from_grad = after_key + key_state, after_grad + grad_state
            s_left[c, j] = enc(from_key)
            s_left[c, PIECE + j] = enc(from_grad)
            base[0, h] = -from_key
            base[1, h] = after_grad
        go_left(c).start()

    def owner_stage(c):
        @pl.when(z > 0)
        def _():
            go_right(c).wait_recv()

        @pl.when(z < nz - 1)
        def _():
            go_left(c).wait_recv()

        for j in range(PIECE):
            h, i = mine * group + c * PIECE + j, c * PIECE + j
            key_state, grad_state = states(h)
            before_key, after_grad = dec(r_right[c, j]), dec(r_left[c, PIECE + j])
            base[0, h] = before_key
            base[1, h] = after_grad
            sums = (
                before_key + key_state + dec(r_left[c, j]),
                dec(r_right[c, PIECE + j]) + grad_state + after_grad,
            )
            for s in range(2):
                own[s, i] = sums[s]
                total[s, i] = sums[s]
                carried[s, i] = jnp.zeros((DK, DK), jnp.float32)
                s_seq[0, c, s * PIECE + j] = enc(sums[s])
        go_seq(0, c).start()

    def seq_stage(r, c):
        go_seq(r - 1, c).wait_recv()
        partner_earlier = later_bit(r - 1).astype(jnp.float32)
        for j in range(PIECE):
            h, i = mine * group + c * PIECE + j, c * PIECE + j
            got_key, got_grad = dec(r_seq[r - 1, c, j]), dec(r_seq[r - 1, c, PIECE + j])
            new_key = carried[0, i] + got_key * partner_earlier
            new_grad = carried[1, i] + got_grad * (1.0 - partner_earlier)
            if r < rounds:
                carried[0, i] = new_key
                carried[1, i] = new_grad
                total_key, total_grad = total[0, i] + got_key, total[1, i] + got_grad
                total[0, i] = total_key
                total[1, i] = total_grad
                s_seq[r, c, j] = enc(total_key)
                s_seq[r, c, PIECE + j] = enc(total_grad)
            else:
                base[0, h] += new_key
                base[1, h] += new_grad
                result[c, j] = enc(jnp.where(first, new_key + own[0, i], new_key))
                result[c, PIECE + j] = enc(jnp.where(first, new_grad, new_grad + own[1, i]))
        if r < rounds:
            go_seq(r, c).start()
        else:
            @pl.when(first)
            def _():
                back_to_right(result.at[c], c).start()

            @pl.when(last)
            def _():
                back_to_left(result.at[c], c).start()

    def relay_left(c):
        back_to_left(r_back.at[1, c], c).wait_recv()

        @pl.when(z > 0)
        def _():
            back_to_left(r_back.at[1, c], c).start()

    def relay_right(c):
        back_to_right(r_back.at[0, c], c).wait_recv()

        @pl.when(z < nz - 1)
        def _():
            back_to_right(r_back.at[0, c], c).start()

    rows = q.shape[0]
    causal = lax.broadcasted_iota(jnp.int32, (rows, rows), 0) >= lax.broadcasted_iota(jnp.int32, (rows, rows), 1)

    def finish(g, c):
        for j in range(PIECE):
            h = g * group + c * PIECE + j
            qh, kh, vh, oh = block(q, h), block(k, h), block(v, h), block(o, h)
            prefix_high, prefix_low = split(base[0, h] + dec(r_back[g, c, j]))
            suffix_high, suffix_low = split(base[1, h] + dec(r_back[g, c, PIECE + j]))
            weights_a = jnp.where(causal, dot(oh, vh, NT), 0.0).astype(jnp.bfloat16)
            weights_b = jnp.where(causal, dot(qh, kh, NT), 0.0).astype(jnp.bfloat16)
            grad_q = dot(weights_a, kh, NN) + dot(oh, prefix_high, NT) + dot(oh, prefix_low, NT)
            grad_k = dot(weights_a, qh, TN) + dot(vh, suffix_high, NT) + dot(vh, suffix_low, NT)
            grad_v = dot(weights_b, oh, TN) + dot(kh, suffix_high, NN) + dot(kh, suffix_low, NN)
            columns = pl.ds(pl.multiple_of(h * DK, DK), DK)
            gq[:, columns] = grad_q.astype(jnp.bfloat16)
            gk[:, columns] = grad_k.astype(jnp.bfloat16)
            gv[:, columns] = grad_v.astype(jnp.bfloat16)

    def valid(c):
        return (c >= 0) & (c < pieces)

    def step(t, carry):
        cl = t - SKEW * (gathered + rounds + nz - 1 - z)

        @pl.when((z < nz - 1) & valid(cl))
        def _():
            relay_left(cl)

        cr = t - SKEW * (gathered + rounds + z)

        @pl.when((z > 0) & valid(cr))
        def _():
            relay_right(cr)

        for r in reversed(range(1, rounds + 1)):
            cs = t - SKEW * (gathered + r)

            @pl.when((first | last) & valid(cs))
            def _():
                seq_stage(r, cs)

        co = t - SKEW * gathered

        @pl.when((first | last) & valid(co))
        def _():
            owner_stage(co)

        c_right, c_left = t - SKEW * z, t - SKEW * (nz - 1 - z)

        @pl.when((z < nz - 1) & valid(c_right))
        def _():
            right_stage(c_right)

        @pl.when((z > 0) & valid(c_left))
        def _():
            left_stage(c_left)

        @pl.when(valid(cr))
        def _():
            finish(0, cr)

        @pl.when(valid(cl))
        def _():
            finish(1, cl)

        return carry

    lax.fori_loop(0, pieces + SKEW * (2 * gathered + rounds), step, 0)

    def drain(c, carry):
        @pl.when(z < nz - 1)
        def _():
            go_right(c).wait_send()
            back_to_right(r_back.at[0, c], c).wait_send()

        @pl.when(z > 0)
        def _():
            go_left(c).wait_send()
            back_to_left(r_back.at[1, c], c).wait_send()

        @pl.when(first | last)
        def _():
            for r in range(rounds):
                go_seq(r, c).wait_send()

        return carry

    lax.fori_loop(0, pieces, drain, 0)


def body(ns, nz, queries, keys, values, grad_out):
    heads = queries.shape[1] // DK
    group = heads // 2
    pieces = group // PIECE
    rounds = ns.bit_length() - 1
    moved = (pieces, 2 * PIECE, DK, DK)

    def bf(*lead):
        return pltpu.VMEM(lead + moved, jnp.bfloat16)

    def f32(count):
        return pltpu.VMEM((2, count, DK, DK), jnp.float32)

    by_piece = pltpu.SemaphoreType.DMA((pieces,))
    by_half = pltpu.SemaphoreType.DMA((2, pieces))
    by_round = pltpu.SemaphoreType.DMA((rounds, pieces))
    return pl.pallas_call(
        functools.partial(kernel, ns, nz),
        out_shape=[jax.ShapeDtypeStruct(queries.shape, jnp.bfloat16)] * 3,
        in_specs=[pl.BlockSpec(memory_space=pltpu.VMEM)] * 4,
        out_specs=[pl.BlockSpec(memory_space=pltpu.VMEM)] * 3,
        scratch_shapes=[
            f32(heads), bf(), bf(), bf(), bf(), f32(group), f32(group), f32(group),
            bf(rounds), bf(rounds), bf(), bf(2),
            by_piece, by_piece, by_piece, by_piece, by_round, by_round, by_half, by_half,
        ],
        compiler_params=pltpu.CompilerParams(
            collective_id=0, has_side_effects=True, vmem_limit_bytes=48 * 1024 * 1024
        ),
    )(queries, keys, values, grad_out)


def solution(mesh):
    ns, nz = mesh.shape["seq"], mesh.shape["head"]
    spec = P(("seq", "head"), None)
    return jax.shard_map(
        functools.partial(body, ns, nz), mesh=mesh, in_specs=(spec,) * 4, out_specs=(spec,) * 3, check_vma=False
    )
```

```python
import functools

import jax
import jax.numpy as jnp
from jax import lax
from jax.experimental import pallas as pl
from jax.experimental.pallas import tpu as pltpu
from jax.sharding import PartitionSpec as P

DK = 128
PIECE = 1
SKEW = 3
MESH = pl.DeviceIdType.MESH
NT = (((1,), (1,)), ((), ()))
TN = (((0,), (0,)), ((), ()))
NN = (((1,), (0,)), ((), ()))


def dot(left, right, dims):
    return lax.dot_general(left, right, dims, preferred_element_type=jnp.float32)


def enc(x):
    return (x * jnp.abs(x) * (x * x)).astype(jnp.bfloat16)


def dec(y):
    y = y.astype(jnp.float32)
    root = jnp.sqrt(jnp.sqrt(jnp.abs(y)))
    return jnp.where(y < 0, -root, root)


def split(x):
    high = x.astype(jnp.bfloat16)
    return high, (x - high.astype(jnp.float32)).astype(jnp.bfloat16)


def kernel(
    ns, nz, q, k, v, o, gq, gk, gv,
    base, s_right, r_right, s_left, r_left, own, total, carried, s_seq, r_seq, result, r_back,
    right_s, right_r, left_s, left_r, seq_s, seq_r, back_s, back_r,
):
    n, z = lax.axis_index("seq"), lax.axis_index("head")
    rounds = ns.bit_length() - 1
    group = base.shape[1] // 2
    mine = (z == nz - 1).astype(jnp.int32)
    pieces = r_right.shape[0]
    first, last = z == 0, z == nz - 1
    gathered = nz - 1

    def later_bit(r):
        return lax.rem(lax.div(n, 1 << r), 2)

    def partner(r):
        return n + (1 - 2 * later_bit(r)) * (1 << r)

    def remote(src, dst, send, recv, where):
        return pltpu.make_async_remote_copy(
            src_ref=src, dst_ref=dst, send_sem=send, recv_sem=recv, device_id=where, device_id_type=MESH
        )

    def go_right(c):
        return remote(s_right.at[c], r_right.at[c], right_s.at[c], right_r.at[c], {"head": z + 1})

    def go_left(c):
        return remote(s_left.at[c], r_left.at[c], left_s.at[c], left_r.at[c], {"head": z - 1})

    def go_seq(r, c):
        return remote(s_seq.at[r, c], r_seq.at[r, c], seq_s.at[r, c], seq_r.at[r, c], {"seq": partner(r)})

    def back_to_left(src, c):
        return remote(src, r_back.at[1, c], back_s.at[1, c], back_r.at[1, c], {"head": z - 1})

    def back_to_right(src, c):
        return remote(src, r_back.at[0, c], back_s.at[0, c], back_r.at[0, c], {"head": z + 1})

    barrier = pltpu.get_barrier_semaphore()

    @pl.when(z > 0)
    def _():
        pl.semaphore_signal(barrier, inc=1, device_id={"head": z - 1}, device_id_type=MESH)

    @pl.when(z < nz - 1)
    def _():
        pl.semaphore_signal(barrier, inc=1, device_id={"head": z + 1}, device_id_type=MESH)

    for r in range(rounds):
        pl.semaphore_signal(barrier, inc=1, device_id={"seq": partner(r)}, device_id_type=MESH)

    @pl.when(first)
    def _():
        r_right[...] = jnp.zeros_like(r_right)

    @pl.when(last)
    def _():
        r_left[...] = jnp.zeros_like(r_left)

    @pl.when(first)
    def _():
        r_back[0] = jnp.zeros(r_back.shape[1:], r_back.dtype)

    @pl.when(last)
    def _():
        r_back[1] = jnp.zeros(r_back.shape[1:], r_back.dtype)

    neighbours = (z > 0).astype(jnp.int32) + (z < nz - 1).astype(jnp.int32)
    pl.semaphore_wait(barrier, rounds + neighbours)

    def block(ref, h):
        return ref[:, pl.ds(pl.multiple_of(h * DK, DK), DK)]

    def states(h):
        return dot(block(k, h), block(v, h), TN), dot(block(q, h), block(o, h), TN)

    def right_stage(c):
        fresh = [states(group + c * PIECE + j) for j in range(PIECE)]

        @pl.when(z > 0)
        def _():
            go_right(c).wait_recv()

        for j in range(PIECE):
            h = group + c * PIECE + j
            key_state, grad_state = fresh[j]
            before_key, before_grad = dec(r_right[c, j]), dec(r_right[c, PIECE + j])
            upto_key, upto_grad = before_key + key_state, before_grad + grad_state
            s_right[c, j] = enc(upto_key)
            s_right[c, PIECE + j] = enc(upto_grad)
            base[0, h] = before_key
            base[1, h] = -upto_grad
        go_right(c).start()

    def left_stage(c):
        fresh = [states(c * PIECE + j) for j in range(PIECE)]

        @pl.when(z < nz - 1)
        def _():
            go_left(c).wait_recv()

        for j in range(PIECE):
            h = c * PIECE + j
            key_state, grad_state = fresh[j]
            after_key, after_grad = dec(r_left[c, j]), dec(r_left[c, PIECE + j])
            from_key, from_grad = after_key + key_state, after_grad + grad_state
            s_left[c, j] = enc(from_key)
            s_left[c, PIECE + j] = enc(from_grad)
            base[0, h] = -from_key
            base[1, h] = after_grad
        go_left(c).start()

    def owner_stage(c):
        fresh = [states(mine * group + c * PIECE + j) for j in range(PIECE)]

        @pl.when(z > 0)
        def _():
            go_right(c).wait_recv()

        @pl.when(z < nz - 1)
        def _():
            go_left(c).wait_recv()

        for j in range(PIECE):
            h, i = mine * group + c * PIECE + j, c * PIECE + j
            key_state, grad_state = fresh[j]
            before_key, after_grad = dec(r_right[c, j]), dec(r_left[c, PIECE + j])
            base[0, h] = before_key
            base[1, h] = after_grad
            sums = (
                before_key + key_state + dec(r_left[c, j]),
                dec(r_right[c, PIECE + j]) + grad_state + after_grad,
            )
            for s in range(2):
                own[s, i] = sums[s]
                total[s, i] = sums[s]
                carried[s, i] = jnp.zeros((DK, DK), jnp.float32)
                s_seq[0, c, s * PIECE + j] = enc(sums[s])
        go_seq(0, c).start()

    def seq_stage(r, c):
        go_seq(r - 1, c).wait_recv()
        partner_earlier = later_bit(r - 1).astype(jnp.float32)
        for j in range(PIECE):
            h, i = mine * group + c * PIECE + j, c * PIECE + j
            got_key, got_grad = dec(r_seq[r - 1, c, j]), dec(r_seq[r - 1, c, PIECE + j])
            new_key = carried[0, i] + got_key * partner_earlier
            new_grad = carried[1, i] + got_grad * (1.0 - partner_earlier)
            if r < rounds:
                carried[0, i] = new_key
                carried[1, i] = new_grad
                total_key, total_grad = total[0, i] + got_key, total[1, i] + got_grad
                total[0, i] = total_key
                total[1, i] = total_grad
                s_seq[r, c, j] = enc(total_key)
                s_seq[r, c, PIECE + j] = enc(total_grad)
            else:
                base[0, h] += new_key
                base[1, h] += new_grad
                result[c, j] = enc(jnp.where(first, new_key + own[0, i], new_key))
                result[c, PIECE + j] = enc(jnp.where(first, new_grad, new_grad + own[1, i]))
        if r < rounds:
            go_seq(r, c).start()
        else:
            @pl.when(first)
            def _():
                back_to_right(result.at[c], c).start()

            @pl.when(last)
            def _():
                back_to_left(result.at[c], c).start()

    def relay_left(c):
        back_to_left(r_back.at[1, c], c).wait_recv()

        @pl.when(z > 0)
        def _():
            back_to_left(r_back.at[1, c], c).start()

    def relay_right(c):
        back_to_right(r_back.at[0, c], c).wait_recv()

        @pl.when(z < nz - 1)
        def _():
            back_to_right(r_back.at[0, c], c).start()

    rows = q.shape[0]
    causal = lax.broadcasted_iota(jnp.int32, (rows, rows), 0) >= lax.broadcasted_iota(jnp.int32, (rows, rows), 1)

    def finish(g, c):
        for j in range(PIECE):
            h = g * group + c * PIECE + j
            qh, kh, vh, oh = block(q, h), block(k, h), block(v, h), block(o, h)
            prefix_high, prefix_low = split(base[0, h] + dec(r_back[g, c, j]))
            suffix_high, suffix_low = split(base[1, h] + dec(r_back[g, c, PIECE + j]))
            weights_a = jnp.where(causal, dot(oh, vh, NT), 0.0).astype(jnp.bfloat16)
            weights_b = jnp.where(causal, dot(qh, kh, NT), 0.0).astype(jnp.bfloat16)
            grad_q = dot(weights_a, kh, NN) + dot(oh, prefix_high, NT) + dot(oh, prefix_low, NT)
            grad_k = dot(weights_a, qh, TN) + dot(vh, suffix_high, NT) + dot(vh, suffix_low, NT)
            grad_v = dot(weights_b, oh, TN) + dot(kh, suffix_high, NN) + dot(kh, suffix_low, NN)
            columns = pl.ds(pl.multiple_of(h * DK, DK), DK)
            gq[:, columns] = grad_q.astype(jnp.bfloat16)
            gk[:, columns] = grad_k.astype(jnp.bfloat16)
            gv[:, columns] = grad_v.astype(jnp.bfloat16)

    def valid(c):
        return (c >= 0) & (c < pieces)

    def step(t, carry):
        cl = t - SKEW * (gathered + rounds + nz - 1 - z)

        @pl.when((z < nz - 1) & valid(cl))
        def _():
            relay_left(cl)

        cr = t - SKEW * (gathered + rounds + z)

        @pl.when((z > 0) & valid(cr))
        def _():
            relay_right(cr)

        for r in reversed(range(1, rounds + 1)):
            cs = t - SKEW * (gathered + r)

            @pl.when((first | last) & valid(cs))
            def _():
                seq_stage(r, cs)

        co = t - SKEW * gathered

        @pl.when((first | last) & valid(co))
        def _():
            owner_stage(co)

        c_right, c_left = t - SKEW * z, t - SKEW * (nz - 1 - z)

        @pl.when((z < nz - 1) & valid(c_right))
        def _():
            right_stage(c_right)

        @pl.when((z > 0) & valid(c_left))
        def _():
            left_stage(c_left)

        @pl.when(valid(cr))
        def _():
            finish(0, cr)

        @pl.when(valid(cl))
        def _():
            finish(1, cl)

        return carry

    lax.fori_loop(0, pieces + SKEW * (2 * gathered + rounds), step, 0)

    def drain(c, carry):
        @pl.when(z < nz - 1)
        def _():
            go_right(c).wait_send()
            back_to_right(r_back.at[0, c], c).wait_send()

        @pl.when(z > 0)
        def _():
            go_left(c).wait_send()
            back_to_left(r_back.at[1, c], c).wait_send()

        @pl.when(first | last)
        def _():
            for r in range(rounds):
                go_seq(r, c).wait_send()

        return carry

    lax.fori_loop(0, pieces, drain, 0)


def body(ns, nz, queries, keys, values, grad_out):
    heads = queries.shape[1] // DK
    group = heads // 2
    pieces = group // PIECE
    rounds = ns.bit_length() - 1
    moved = (pieces, 2 * PIECE, DK, DK)

    def bf(*lead):
        return pltpu.VMEM(lead + moved, jnp.bfloat16)

    def f32(count):
        return pltpu.VMEM((2, count, DK, DK), jnp.float32)

    by_piece = pltpu.SemaphoreType.DMA((pieces,))
    by_half = pltpu.SemaphoreType.DMA((2, pieces))
    by_round = pltpu.SemaphoreType.DMA((rounds, pieces))
    return pl.pallas_call(
        functools.partial(kernel, ns, nz),
        out_shape=[jax.ShapeDtypeStruct(queries.shape, jnp.bfloat16)] * 3,
        in_specs=[pl.BlockSpec(memory_space=pltpu.VMEM)] * 4,
        out_specs=[pl.BlockSpec(memory_space=pltpu.VMEM)] * 3,
        scratch_shapes=[
            f32(heads), bf(), bf(), bf(), bf(), f32(group), f32(group), f32(group),
            bf(rounds), bf(rounds), bf(), bf(2),
            by_piece, by_piece, by_piece, by_piece, by_round, by_round, by_half, by_half,
        ],
        compiler_params=pltpu.CompilerParams(
            collective_id=0, has_side_effects=True, vmem_limit_bytes=48 * 1024 * 1024
        ),
    )(queries, keys, values, grad_out)


def solution(mesh):
    ns, nz = mesh.shape["seq"], mesh.shape["head"]
    spec = P(("seq", "head"), None)
    return jax.shard_map(
        functools.partial(body, ns, nz), mesh=mesh, in_specs=(spec,) * 4, out_specs=(spec,) * 3, check_vma=False
    )
```
